512 devices in a mesh: node: 32 (over z, y_lo, core), local: 16 (over x, y_hi).
Axes of the slice: x: 4, y: 8 (y_hi: 4, y_lo: 2; y = y_hi * 2 + y_lo), z: 8, core: 2. Of those that a mesh axis runs over, the one named last changes fastest.
Arguments:
- tokens: bfloat16 [2048, 4096], P('local', 'node'), may hold values from -6 to 6
- cotangent: bfloat16 [2048, 14336], P('local', 'node'), may hold values from -0.125 to 0.125
- gate_weight: bfloat16 [4096, 14336], P('local', 'node'), may hold values from -0.09375 to 0.09375
- up_weight: bfloat16 [4096, 14336], P('local', 'node'), may hold values from -0.09375 to 0.09375
- gate_first: bfloat16 [4096, 14336], P('local', 'node'), may hold values from -3 to 3
- up_first: bfloat16 [4096, 14336], P('local', 'node'), may hold values from -3 to 3
- gate_second: bfloat16 [4096, 14336], P('local', 'node'), may hold values from 0.00029945374 to 0.029907227
- up_second: bfloat16 [4096, 14336], P('local', 'node'), may hold values from 0.00029945374 to 0.029907227
Outputs:
- input_grad: bfloat16 [2048, 4096], P('local', 'node')
- gate_new: bfloat16 [4096, 14336], P('local', 'node')
- up_new: bfloat16 [4096, 14336], P('local', 'node')
- gate_first_new: bfloat16 [4096, 14336], P('local', 'node')
- up_first_new: bfloat16 [4096, 14336], P('local', 'node')
- gate_second_new: bfloat16 [4096, 14336], P('local', 'node')
- up_second_new: bfloat16 [4096, 14336], P('local', 'node')
The draws below stay inside these ranges and needn't reach their ends.
All inputs are finite; a program needn't handle non-finite values.
Results may differ from the reference program's by a relative error of at most 0.0049.
Values may be sent and summed in bfloat16 or wider, within the bound.
A program may use at most 64 MiB of HBM per device.

```python
import math
import jax
import jax.numpy as jnp

D = 4096
FF = 14336
TOKENS = 2048


def block_levels(stream_key, extent, split, low, high):
    def one(axis_at, parts):
        steps = jax.random.uniform(jax.random.fold_in(jax.random.fold_in(stream_key, 6), axis_at), (parts,), jnp.float32, low / len(split), high / len(split))
        return jnp.repeat(jnp.exp(steps), extent[axis_at] // parts).reshape((-1,) + (1,) * (len(extent) - axis_at - 1))

    gain = one(*split[0])
    for cut in split[1:]:
        gain = gain * one(*cut)
    return gain


def normal_values(stream_key, shape, deviation, most, split=(), held_as=jnp.bfloat16):
    level = block_levels(stream_key, shape, split, -0.22, 0.18) if split else 1.0
    result = jax.random.normal(stream_key, shape, jnp.float32) * deviation * level
    return jnp.minimum(jnp.maximum(result, -most), most).astype(held_as)


def setup_inputs(seed: int = 0) -> dict:
    streams_of = jax.random.split(jax.random.key(seed), 9)
    return {
        "tokens": normal_values(streams_of[0], (TOKENS, D), 1.0, 6.0, ((0, 16), (1, 32))),
        "cotangent": normal_values(streams_of[1], (TOKENS, FF), TOKENS ** -0.5, 0.125, ((0, 16), (1, 32))),
        "gate_weight": normal_values(streams_of[2], (D, FF), D ** -0.5, 0.09375, ((0, 16), (1, 32))),
        "up_weight": normal_values(streams_of[3], (D, FF), D ** -0.5, 0.09375, ((0, 16), (1, 32))),
        "gate_first": normal_values(streams_of[4], (D, FF), 0.5, 3.0, ((0, 16), (1, 32))),
        "up_first": normal_values(streams_of[5], (D, FF), 0.5, 3.0, ((0, 16), (1, 32))),
        "gate_second": jnp.clip(jnp.exp(math.log(0.029907227) - 4.6038955 * jax.random.uniform(streams_of[6], (D, FF), jnp.float32) ** block_levels(streams_of[6], (D, FF), ((0, 16), (1, 32)), -0.2, 0.2)), 0.00029945374, 0.029907227).astype(jnp.bfloat16),
        "up_second": jnp.clip(jnp.exp(math.log(0.029907227) - 4.6038955 * jax.random.uniform(streams_of[7], (D, FF), jnp.float32) ** block_levels(streams_of[7], (D, FF), ((0, 16), (1, 32)), -0.2, 0.2)), 0.00029945374, 0.029907227).astype(jnp.bfloat16),
    }


first_decay = 0.9
second_decay = 0.999
learn_rate = 0.001
adam_eps = 1e-08
step_count = 10

def adam_update(weight, first, second, grad):
    first_new = first_decay * first.astype(jnp.float32) + (1.0 - first_decay) * grad
    second_new = second_decay * second.astype(jnp.float32) + (1.0 - second_decay) * grad * grad
    first_hat = first_new / (1.0 - first_decay ** step_count)
    second_hat = second_new / (1.0 - second_decay ** step_count)
    weight_new = weight.astype(jnp.float32) - learn_rate * first_hat / (jnp.sqrt(second_hat) + adam_eps)
    return (weight_new.astype(jnp.bfloat16), first_new.astype(jnp.bfloat16), second_new.astype(jnp.bfloat16))

def reference(tokens, cotangent, gate_weight, up_weight, gate_first, up_first, gate_second, up_second):
    gate_pre = jnp.dot(tokens, gate_weight, preferred_element_type=jnp.float32)
    up_pre = jnp.dot(tokens, up_weight, preferred_element_type=jnp.float32)
    sigmoid_gate = jax.nn.sigmoid(gate_pre)
    upstream = cotangent.astype(jnp.float32)
    gate_grad = (upstream * up_pre * sigmoid_gate * (1.0 + gate_pre * (1.0 - sigmoid_gate))).astype(jnp.bfloat16)
    up_grad = (upstream * gate_pre * sigmoid_gate).astype(jnp.bfloat16)
    input_grad = jnp.dot(gate_grad, gate_weight.T, preferred_element_type=jnp.float32)
    input_grad = input_grad + jnp.dot(up_grad, up_weight.T, preferred_element_type=jnp.float32)
    gate_wgrad = jnp.dot(tokens.T, gate_grad, preferred_element_type=jnp.float32)
    up_wgrad = jnp.dot(tokens.T, up_grad, preferred_element_type=jnp.float32)
    gate_new, gate_first_new, gate_second_new = adam_update(gate_weight, gate_first, gate_second, gate_wgrad)
    up_new, up_first_new, up_second_new = adam_update(up_weight, up_first, up_second, up_wgrad)
    return (input_grad.astype(jnp.bfloat16), gate_new, up_new, gate_first_new, up_first_new, gate_second_new, up_second_new)
```

```python
import functools

import jax
import jax.numpy as jnp
from jax import lax
from jax.experimental import pallas as pl
from jax.experimental.pallas import tpu as pltpu
from jax.sharding import PartitionSpec as P

first_decay = 0.9
second_decay = 0.999
learn_rate = 0.001
adam_eps = 1e-08
step_count = 10

MESH = pl.DeviceIdType.MESH
bf16, f32 = jnp.bfloat16, jnp.float32

NT = 2
TB = 128 // NT
H = TB // 2
CHUNKS = ((0, 1), (2, 3))
NF = len(CHUNKS)
SEMS = 256


def tile_width(k):
    return 256 if k < 3 else 128


WIDTH = tuple(sum(tile_width(k) for k in tiles) for tiles in CHUNKS)


def adam_update(weight, first, second, grad):
    first_new = first_decay * first.astype(jnp.float32) + (1.0 - first_decay) * grad
    second_new = second_decay * second.astype(jnp.float32) + (1.0 - second_decay) * grad * grad
    first_hat = first_new / (1.0 - first_decay**step_count)
    second_hat = second_new / (1.0 - second_decay**step_count)
    weight_new = weight.astype(jnp.float32) - learn_rate * first_hat / (
        jnp.sqrt(second_hat) + adam_eps
    )
    return (
        weight_new.astype(jnp.bfloat16),
        first_new.astype(jnp.bfloat16),
        second_new.astype(jnp.bfloat16),
    )


def tiles_of(f):
    at = 0
    for k in CHUNKS[f]:
        yield k, at
        at += tile_width(k)


def kernel(tok, cot, gw, uw, dx_out, gg_out, ug_out, *scratch):
    names = list(SCRATCH)
    s = dict(zip(names, scratch))
    send, recv = s["send"], s["recv"]
    node, local = lax.axis_index("node"), lax.axis_index("local")
    z, w, c = node // 4, (node // 2) % 2, node % 2
    a, b = local // 4, local % 4

    def dev(x=a, y=b, zz=z, ww=w, cc=c):
        return (zz * 4 + ww * 2 + cc, x * 4 + y)

    right = {"x": dev(x=(a + 1) % 4), "y": dev(y=(b + 1) % 4)}
    left = {"x": dev(x=(a + 3) % 4), "y": dev(y=(b + 3) % 4)}
    partner = dev(cc=1 - c)
    is_sink = (z % 2) == (b // 2)

    count = [0]
    unsent = []

    def take(n=1):
        at = count[0]
        count[0] += n
        assert count[0] <= SEMS
        return at

    def put(src, dst, to, sem=None, sem_at=None):
        i = take() if sem is None else sem
        j = i if sem_at is None else sem_at
        copy = pltpu.make_async_remote_copy(
            src_ref=src, dst_ref=dst, send_sem=send.at[i], recv_sem=recv.at[j],
            device_id=to, device_id_type=MESH,
        )
        copy.start()
        unsent.append(copy)
        return copy

    def gather_start(buf, axis, half):
        lo, hi = pl.ds(0, half), pl.ds(half, half)
        r1 = put(buf.at[0, lo], buf.at[3, lo], right[axis])
        l1 = put(buf.at[0, hi], buf.at[1, hi], left[axis])
        r2 = put(buf.at[0, hi], buf.at[3, hi], right[axis])
        l2 = put(buf.at[0, lo], buf.at[1, lo], left[axis])
        return [buf, axis, half, r1, l1, r2, l2]

    def gather_relay(g):
        buf, axis, half, r1, l1, r2, l2 = g
        lo, hi = pl.ds(0, half), pl.ds(half, half)
        r1.wait_recv()
        r3 = put(buf.at[3, lo], buf.at[2, lo], right[axis])
        l1.wait_recv()
        l3 = put(buf.at[1, hi], buf.at[2, hi], left[axis])
        g += [r3, l3]

    def gather_finish(g):
        for copy in g[5:]:
            copy.wait_recv()

    def reduce_start(part, keep, mid_left, mid_right, from_left, from_right, axis, half):
        lo, hi = pl.ds(0, half), pl.ds(half, half)
        r1 = put(part.at[1, lo], mid_left, right[axis])
        l1 = put(part.at[1, hi], mid_right, left[axis])
        r2 = put(part.at[0, hi], from_left.at[hi], right[axis])
        l2 = put(part.at[2, lo], from_right.at[lo], left[axis])
        return [part, keep, mid_left, mid_right, from_left, from_right, axis, half, r1, l1, r2, l2]

    def reduce_relay(g):
        part, keep, mid_left, mid_right, from_left, from_right, axis, half, r1, l1, r2, l2 = g
        lo, hi = pl.ds(0, half), pl.ds(half, half)
        r1.wait_recv()
        part[0, :half] = (keep[0] + mid_left[...].astype(f32)).astype(bf16)
        r3 = put(part.at[0, lo], from_left.at[lo], right[axis])
        l1.wait_recv()
        part[2, half:] = (keep[1] + mid_right[...].astype(f32)).astype(bf16)
        l3 = put(part.at[2, hi], from_right.at[hi], left[axis])
        g += [r3, l3]

    def reduce_finish(g):
        for copy in g[10:]:
            copy.wait_recv()

    peers = [right["x"], left["x"], partner]
    peers += [dev(zz=(z + k) % 8) for k in range(1, 8)]
    peers += [dev(y=(b + k) % 4, ww=w) for k in range(1, 4)]
    peers += [dev(y=(b + k) % 4, ww=1 - w) for k in range(4)]
    barrier = pltpu.get_barrier_semaphore()
    for peer in peers:
        pl.semaphore_signal(barrier, inc=1, device_id=peer, device_id_type=MESH)
    pl.semaphore_wait(barrier, len(peers))

    held, X = s["held"], s["X"]
    home = 2 * (z % 2) + w
    slot = (b - home + 4) % 4
    held_sem = take(4)
    tok_sem = take(2)
    for wd in range(2):
        own = (home == b) & (w == wd)

        def tok_remote(to=dev(y=home, ww=wd), i=tok_sem + wd):
            return pltpu.make_async_remote_copy(
                src_ref=tok, dst_ref=held.at[slot], send_sem=send.at[i],
                recv_sem=recv.at[held_sem + slot], device_id=to, device_id_type=MESH,
            )

        @pl.when(own)
        def _():
            pltpu.make_async_copy(tok, held.at[0], recv.at[held_sem]).start()

        @pl.when(jnp.logical_not(own))
        def _():
            tok_remote().start()

    W = [s[f"W{f}"] for f in range(NF)]
    w_gather = []
    for f in range(NF):
        for k, at in tiles_of(f):
            if k < 3:
                W[f][0, :, at:at + 128] = gw[:, 128 * k:128 * k + 128]
                W[f][0, :, at + 128:at + 256] = uw[:, 128 * k:128 * k + 128]
            else:
                W[f][0, :, at:at + 128] = jnp.concatenate([gw[:, 384:448], uw[:, 384:448]], axis=1)
        w_gather.append(gather_start(W[f], "x", 128))

    column = (z // 2 - a + 4) % 4
    z_sem = take(4 * NT)
    z_send = take(7 * NT)

    def z_dst(h, j):
        return X.at[h, :, :, pl.ds(pl.multiple_of((2 * j + c) * 128, 128), 128)]

    def z_copy(h, k):
        return pltpu.make_async_remote_copy(
            src_ref=held.at[:, pl.ds(h * TB, TB)], dst_ref=z_dst(h, column),
            send_sem=send.at[z_send + h * 7 + k - 1], recv_sem=recv.at[z_sem + 4 * h + column],
            device_id=dev(zz=(z + k) % 8), device_id_type=MESH,
        )

    @pl.when(is_sink)
    def _():
        for r in range(4):
            pltpu.make_async_copy(tok, held.at[r], recv.at[held_sem + r]).wait()
        for h in range(NT):
            pltpu.make_async_copy(
                held.at[:, pl.ds(h * TB, TB)], z_dst(h, column), recv.at[z_sem + 4 * h + column]
            ).start()
            for k in (1, 7, 2, 6, 3, 5, 4):
                z_copy(h, k).start()

    def x_relay(h):
        copies = []
        for j in range(4):
            pltpu.make_async_copy(
                held.at[:, pl.ds(h * TB, TB)], z_dst(h, j), recv.at[z_sem + 4 * h + j]
            ).wait()
            copies.append(put(z_dst(h, j), z_dst(h, j), partner))
        return copies

    units = [(h, f) for h in range(NT) for f in range(NF)]
    pre_reduce, g_gather, w_reduce = {}, {}, {}

    def project(h, f):
        x = X[h].reshape(4 * TB, 1024)
        out = jnp.dot(x, W[f][...].reshape(1024, WIDTH[f]), preferred_element_type=f32)
        out = out.reshape(4, TB, WIDTH[f])
        s[f"own{f}"][h] = out[0]
        part, keep = s[f"part{f}"].at[h], s[f"keep{f}"].at[h]
        part[1] = out[2].astype(bf16)
        part[0, H:] = out[1, H:].astype(bf16)
        part[2, :H] = out[3, :H].astype(bf16)
        keep[0] = out[1, :H]
        keep[1] = out[3, H:]
        pre_reduce[h, f] = reduce_start(
            part, keep, s[f"midl{f}"].at[h], s[f"midr{f}"].at[h],
            s[f"finl{f}"].at[h], s[f"finr{f}"].at[h], "y", H,
        )

    def pointwise(gp, up, ct):
        sg = jax.nn.sigmoid(gp)
        cs = ct * sg
        return cs * up * (1.0 + gp * (1.0 - sg)), cs * gp

    def gate(h, f):
        reduce_finish(pre_reduce[h, f])
        pre = s[f"own{f}"][h] + s[f"finl{f}"][h].astype(f32) + s[f"finr{f}"][h].astype(f32)
        rows = slice(h * TB, h * TB + TB)
        G = s[f"G{f}"]
        for k, at in tiles_of(f):
            if k < 3:
                ct = cot[rows, 128 * k:128 * k + 128].astype(f32)
                gg, ug = pointwise(pre[:, at:at + 128], pre[:, at + 128:at + 256], ct)
                G[h, 0, :, at:at + 128] = gg.astype(bf16)
                G[h, 0, :, at + 128:at + 256] = ug.astype(bf16)
            else:
                ct = cot[rows, 384:448].astype(f32)
                ct = jnp.concatenate([ct, ct], axis=1)
                both = pre[:, at:at + 128]
                gg, ug = pointwise(both, pltpu.roll(both, 64, 1), ct)
                lane = lax.broadcasted_iota(jnp.int32, gg.shape, 1)
                G[h, 0, :, at:at + 128] = jnp.where(lane < 64, gg, pltpu.roll(ug, 64, 1)).astype(bf16)
        g_gather[h, f] = gather_start(G.at[h], "y", H)

    acc = s["acc"]

    def input_grad(h, f):
        gather_finish(g_gather[h, f])
        g = s[f"G{f}"][h].reshape(4 * TB, WIDTH[f])
        out = lax.dot_general(
            g, W[f][...].reshape(1024, WIDTH[f]), (((1,), (1,)), ((), ())),
            preferred_element_type=f32,
        )
        for k in range(8):
            if f == 0:
                acc[h, k] = out[:, 128 * k:128 * k + 128]
            else:
                acc[h, k] += out[:, 128 * k:128 * k + 128]

    core_recv, sink_send, sink_recv = (s[n] for n in ("cr", "zs", "zr"))
    core_copies = {}

    def dx_core(h):
        core_copies[h] = []
        for j in range(4):
            core_copies[h].append(put(acc.at[h, 2 * j + 1 - c], core_recv.at[h, j], partner))

    dx_sem = take(8 * NT)
    dx_send = take(4 * NT)

    def sink_copy(h, j):
        zj = 2 * ((a + j) % 4) + b // 2
        k = (z - zj + 8) % 8
        remote = pltpu.make_async_remote_copy(
            src_ref=sink_send.at[h, j], dst_ref=sink_recv.at[h, k],
            send_sem=send.at[dx_send + 4 * h + j], recv_sem=recv.at[dx_sem + 8 * h + k],
            device_id=dev(zz=zj), device_id_type=MESH,
        )
        return zj, remote

    def dx_sinks(h):
        for j in range(4):
            core_copies[h][j].wait_recv()
            sink_send[h, j] = (acc[h, 2 * j + c] + core_recv[h, j]).astype(bf16)
            zj, remote = sink_copy(h, j)

            @pl.when(zj == z)
            def _():
                pltpu.make_async_copy(
                    sink_send.at[h, j], sink_recv.at[h, 0], recv.at[dx_sem + 8 * h]
                ).start()

            @pl.when(zj != z)
            def _():
                remote.start()

    last_send, last_recv = s["ls"], s["lr"]
    out_sem = take(2 * NT)
    out_send = take(4 * NT)

    def out_copy(h, r):
        return pltpu.make_async_remote_copy(
            src_ref=last_send.at[h, pl.ds(r * TB, TB)], dst_ref=last_recv.at[h, w],
            send_sem=send.at[out_send + 4 * h + r], recv_sem=recv.at[out_sem + 2 * h + w],
            device_id=dev(y=(b + r) % 4, ww=b % 2), device_id_type=MESH,
        )

    def dx_spread(h):
        @pl.when(is_sink)
        def _():
            total = None
            for k in range(8):
                pltpu.make_async_copy(
                    sink_send.at[h, 0], sink_recv.at[h, k], recv.at[dx_sem + 8 * h + k]
                ).wait()
                term = sink_recv[h, k].astype(f32)
                total = term if total is None else total + term
            last_send[h] = total
            for r in range(4):
                if r:
                    out_copy(h, r).start()
                else:
                    @pl.when(w == b % 2)
                    def _():
                        pltpu.make_async_copy(
                            last_send.at[h, pl.ds(0, TB)], last_recv.at[h, w],
                            recv.at[out_sem + 2 * h + w],
                        ).start()

                    @pl.when(w != b % 2)
                    def _():
                        out_copy(h, 0).start()

    def dx_finish(h):
        for ww in range(2):
            pltpu.make_async_copy(
                last_send.at[h, pl.ds(0, TB)], last_recv.at[h, ww], recv.at[out_sem + 2 * h + ww]
            ).wait()
        dx_out[h * TB:h * TB + TB] = (last_recv[h, 0] + last_recv[h, 1]).astype(bf16)

    def weight_grad(f):
        g = s[f"G{f}"][...].reshape(512, WIDTH[f])
        for j in (2, 1, 3, 0):
            x = X[:, :, :, 256 * j:256 * j + 256].reshape(512, 256)
            out = lax.dot_general(x, g, (((0,), (0,)), ((), ())), preferred_element_type=f32)
            if j == 2:
                s[f"wp{f}"][1] = out.astype(bf16)
            elif j == 1:
                s[f"wp{f}"][0, 128:] = out[128:].astype(bf16)
                s[f"wk{f}"][0] = out[:128]
            elif j == 3:
                s[f"wp{f}"][2, :128] = out[:128].astype(bf16)
                s[f"wk{f}"][1] = out[128:]
            else:
                s[f"wo{f}"][...] = out
            if j == 3:
                w_reduce[f] = reduce_start(
                    s[f"wp{f}"], s[f"wk{f}"], s[f"wml{f}"], s[f"wmr{f}"], s[f"wfl{f}"], s[f"wfr{f}"], "x", 128
                )

    def weight_finish(f):
        reduce_finish(w_reduce[f])
        total = s[f"wo{f}"][...] + s[f"wfl{f}"][...].astype(f32) + s[f"wfr{f}"][...].astype(f32)
        for k, at in tiles_of(f):
            if k < 3:
                gg_out[:, 128 * k:128 * k + 128] = total[:, at:at + 128]
                ug_out[:, 128 * k:128 * k + 128] = total[:, at + 128:at + 256]
            else:
                both = total[:, at:at + 128]
                gg_out[:, 384:448] = both[:, :64]
                ug_out[:, 384:448] = pltpu.roll(both, 64, 1)[:, :64]

    def ready(copies):
        for copy in copies:
            copy.wait_recv()

    gather_relay(w_gather[0])
    x0 = x_relay(0)
    gather_relay(w_gather[1])
    gather_finish(w_gather[0])
    ready(x0)
    project(0, 0)
    gather_finish(w_gather[1])
    project(0, 1)
    reduce_relay(pre_reduce[0, 0])
    reduce_relay(pre_reduce[0, 1])
    x1 = x_relay(1)
    ready(x1)
    project(1, 0)
    project(1, 1)
    gate(0, 0)
    gate(0, 1)
    gather_relay(g_gather[0, 0])
    gather_relay(g_gather[0, 1])
    reduce_relay(pre_reduce[1, 0])
    reduce_relay(pre_reduce[1, 1])
    input_grad(0, 0)
    input_grad(0, 1)
    dx_core(0)
    gate(1, 0)
    dx_sinks(0)
    gate(1, 1)
    gather_relay(g_gather[1, 0])
    gather_relay(g_gather[1, 1])
    dx_spread(0)
    input_grad(1, 0)
    weight_grad(0)
    input_grad(1, 1)
    dx_core(1)
    weight_grad(1)
    dx_sinks(1)
    reduce_relay(w_reduce[0])
    dx_finish(0)
    reduce_relay(w_reduce[1])
    dx_spread(1)
    weight_finish(0)
    dx_finish(1)
    weight_finish(1)

    for copy in unsent:
        copy.wait_send()
    for wd in range(2):
        @pl.when(jnp.logical_not((home == b) & (w == wd)))
        def _():
            pltpu.make_async_remote_copy(
                src_ref=tok, dst_ref=held.at[slot], send_sem=send.at[tok_sem + wd],
                recv_sem=recv.at[held_sem + slot], device_id=dev(y=home, ww=wd),
                device_id_type=MESH,
            ).wait_send()

    for h in range(NT):
        for j in range(4):
            zj, remote = sink_copy(h, j)

            @pl.when(zj != z)
            def _():
                remote.wait_send()

    @pl.when(is_sink)
    def _():
        for h in range(NT):
            for k in range(1, 8):
                z_copy(h, k).wait_send()
            for r in range(1, 4):
                out_copy(h, r).wait_send()

            @pl.when(w != b % 2)
            def _():
                out_copy(h, 0).wait_send()


def scratch_shapes():
    V = pltpu.VMEM
    shapes = {
        "held": V((4, 128, 128), bf16),
        "X": V((NT, 4, TB, 1024), bf16),
        "acc": V((NT, 8, 4 * TB, 128), f32),
        "cr": V((NT, 4, 4 * TB, 128), f32),
        "zs": V((NT, 4, 4 * TB, 128), bf16),
        "zr": V((NT, 8, 4 * TB, 128), bf16),
        "ls": V((NT, 4 * TB, 128), f32),
        "lr": V((NT, 2, TB, 128), f32),
    }
    for f in range(NF):
        n = WIDTH[f]
        shapes[f"W{f}"] = V((4, 256, n), bf16)
        shapes[f"G{f}"] = V((NT, 4, TB, n), bf16)
        shapes[f"own{f}"] = V((NT, TB, n), f32)
        shapes[f"part{f}"] = V((NT, 3, TB, n), bf16)
        shapes[f"keep{f}"] = V((NT, 2, H, n), f32)
        shapes[f"midl{f}"] = V((NT, H, n), bf16)
        shapes[f"midr{f}"] = V((NT, H, n), bf16)
        shapes[f"finl{f}"] = V((NT, TB, n), bf16)
        shapes[f"finr{f}"] = V((NT, TB, n), bf16)
        shapes[f"wo{f}"] = V((256, n), f32)
        shapes[f"wp{f}"] = V((3, 256, n), bf16)
        shapes[f"wk{f}"] = V((2, 128, n), f32)
        shapes[f"wml{f}"] = V((128, n), bf16)
        shapes[f"wmr{f}"] = V((128, n), bf16)
        shapes[f"wfl{f}"] = V((256, n), bf16)
        shapes[f"wfr{f}"] = V((256, n), bf16)
    shapes["send"] = pltpu.SemaphoreType.DMA((SEMS,))
    shapes["recv"] = pltpu.SemaphoreType.DMA((SEMS,))
    return shapes


SCRATCH = scratch_shapes()


def gradients(tokens, cotangent, gate_weight, up_weight):
    vmem = pl.BlockSpec(memory_space=pltpu.VMEM)
    return pl.pallas_call(
        kernel,
        out_shape=(
            jax.ShapeDtypeStruct((128, 128), bf16),
            jax.ShapeDtypeStruct((256, 448), f32),
            jax.ShapeDtypeStruct((256, 448), f32),
        ),
        in_specs=[vmem] * 4,
        out_specs=(vmem,) * 3,
        scratch_shapes=list(SCRATCH.values()),
        compiler_params=pltpu.CompilerParams(
            collective_id=0, has_side_effects=True, vmem_limit_bytes=48 << 20
        ),
        cost_estimate=pl.CostEstimate(
            flops=2_818_572_288, bytes_accessed=2_000_000, transcendentals=57344
        ),
    )(tokens, cotangent, gate_weight, up_weight)


def shards(tokens, cotangent, gate_weight, up_weight, gate_first, up_first, gate_second, up_second):
    input_grad, gate_wgrad, up_wgrad = gradients(tokens, cotangent, gate_weight, up_weight)
    gate_new, gate_first_new, gate_second_new = adam_update(
        gate_weight, gate_first, gate_second, gate_wgrad
    )
    up_new, up_first_new, up_second_new = adam_update(up_weight, up_first, up_second, up_wgrad)
    return (
        input_grad,
        gate_new,
        up_new,
        gate_first_new,
        up_first_new,
        gate_second_new,
        up_second_new,
    )


def solution(mesh):
    spec = P("local", "node")
    return jax.shard_map(
        shards, mesh=mesh, in_specs=(spec,) * 8, out_specs=(spec,) * 7, check_vma=False
    )
```

```python
import functools

import jax
import jax.numpy as jnp
from jax import lax
from jax.experimental import pallas as pl
from jax.experimental.pallas import tpu as pltpu
from jax.sharding import PartitionSpec as P

first_decay = 0.9
second_decay = 0.999
learn_rate = 0.001
adam_eps = 1e-08
step_count = 10

MESH = pl.DeviceIdType.MESH
bf16, f32 = jnp.bfloat16, jnp.float32

NT = 2
TB = 128 // NT
H = TB // 2
CHUNKS = ((0, 1), (2, 3))
NF = len(CHUNKS)
SEMS = 256


def tile_width(k):
    return 256 if k < 3 else 128


WIDTH = tuple(sum(tile_width(k) for k in tiles) for tiles in CHUNKS)


def adam_update(weight, first, second, grad):
    first_new = first_decay * first.astype(jnp.float32) + (1.0 - first_decay) * grad
    second_new = second_decay * second.astype(jnp.float32) + (1.0 - second_decay) * grad * grad
    first_hat = first_new / (1.0 - first_decay**step_count)
    second_hat = second_new / (1.0 - second_decay**step_count)
    weight_new = weight.astype(jnp.float32) - learn_rate * first_hat / (
        jnp.sqrt(second_hat) + adam_eps
    )
    return (
        weight_new.astype(jnp.bfloat16),
        first_new.astype(jnp.bfloat16),
        second_new.astype(jnp.bfloat16),
    )


def tiles_of(f):
    at = 0
    for k in CHUNKS[f]:
        yield k, at
        at += tile_width(k)


def kernel(tok, cot_t, gw, uw, dx_out, gg_out, ug_out, *scratch):
    names = list(SCRATCH)
    s = dict(zip(names, scratch))
    send, recv = s["send"], s["recv"]
    node, local = lax.axis_index("node"), lax.axis_index("local")
    z, w, c = node // 4, (node // 2) % 2, node % 2
    a, b = local // 4, local % 4

    def dev(x=a, y=b, zz=z, ww=w, cc=c):
        return (zz * 4 + ww * 2 + cc, x * 4 + y)

    right = {"x": dev(x=(a + 1) % 4), "y": dev(y=(b + 1) % 4)}
    left = {"x": dev(x=(a + 3) % 4), "y": dev(y=(b + 3) % 4)}
    partner = dev(cc=1 - c)
    is_sink = (z % 2) == (b // 2)

    count = [0]
    leaving = []

    def take(n=1):
        at = count[0]
        count[0] += n
        assert count[0] <= SEMS
        return at

    def put(src, dst, to, sem=None, sem_at=None):
        i = take() if sem is None else sem
        j = i if sem_at is None else sem_at
        copy = pltpu.make_async_remote_copy(
            src_ref=src, dst_ref=dst, send_sem=send.at[i], recv_sem=recv.at[j],
            device_id=to, device_id_type=MESH,
        )
        copy.start()
        leaving.append(copy.wait_send)
        return copy

    def gather_start(buf, axis, half):
        lo, hi = pl.ds(0, half), pl.ds(half, half)
        r1 = put(buf.at[0, lo], buf.at[3, lo], right[axis])
        l1 = put(buf.at[0, hi], buf.at[1, hi], left[axis])
        r2 = put(buf.at[0, hi], buf.at[3, hi], right[axis])
        l2 = put(buf.at[0, lo], buf.at[1, lo], left[axis])
        return [buf, axis, half, r1, l1, r2, l2]

    def gather_relay(g):
        buf, axis, half, r1, l1, r2, l2 = g
        lo, hi = pl.ds(0, half), pl.ds(half, half)
        r1.wait_recv()
        r3 = put(buf.at[3, lo], buf.at[2, lo], right[axis])
        l1.wait_recv()
        l3 = put(buf.at[1, hi], buf.at[2, hi], left[axis])
        g += [r3, l3]

    def gather_finish(g):
        for copy in g[5:]:
            copy.wait_recv()

    def reduce_start(part, keep, mid_left, mid_right, from_left, from_right, axis, half):
        lo, hi = pl.ds(0, half), pl.ds(half, half)
        r1 = put(part.at[1, lo], mid_left, right[axis])
        l1 = put(part.at[1, hi], mid_right, left[axis])
        r2 = put(part.at[0, hi], from_left.at[hi], right[axis])
        l2 = put(part.at[2, lo], from_right.at[lo], left[axis])
        return [part, keep, mid_left, mid_right, from_left, from_right, axis, half, r1, l1, r2, l2]

    def reduce_relay(g):
        part, keep, mid_left, mid_right, from_left, from_right, axis, half, r1, l1, r2, l2 = g
        lo, hi = pl.ds(0, half), pl.ds(half, half)
        r1.wait_recv()
        part[0, :half] = (keep[0] + mid_left[...].astype(f32)).astype(bf16)
        r3 = put(part.at[0, lo], from_left.at[lo], right[axis])
        l1.wait_recv()
        part[2, half:] = (keep[1] + mid_right[...].astype(f32)).astype(bf16)
        l3 = put(part.at[2, hi], from_right.at[hi], left[axis])
        g += [r3, l3]

    def reduce_finish(g):
        for copy in g[10:]:
            copy.wait_recv()

    peers = [right["x"], left["x"], partner]
    peers += [dev(zz=(z + k) % 8) for k in range(1, 8)]
    peers += [dev(y=(b + k) % 4, ww=w) for k in range(1, 4)]
    peers += [dev(y=(b + k) % 4, ww=1 - w) for k in range(4)]
    barrier = pltpu.get_barrier_semaphore()
    for peer in peers:
        pl.semaphore_signal(barrier, inc=1, device_id=peer, device_id_type=MESH)
    pl.semaphore_wait(barrier, len(peers))

    held, X = s["held"], s["X"]
    home = 2 * (z % 2) + w
    slot = (b - home + 4) % 4
    held_sem = take(4)
    tok_sem = take(2)
    for wd in range(2):
        own = (home == b) & (w == wd)
        away = jnp.logical_not(own)

        def tok_remote(to=dev(y=home, ww=wd), i=tok_sem + wd):
            return pltpu.make_async_remote_copy(
                src_ref=tok, dst_ref=held.at[slot], send_sem=send.at[i],
                recv_sem=recv.at[held_sem + slot], device_id=to, device_id_type=MESH,
            )

        @pl.when(own)
        def _():
            pltpu.make_async_copy(tok, held.at[0], recv.at[held_sem]).start()

        @pl.when(away)
        def _():
            tok_remote().start()

        leaving.append(lambda away=away, copy=tok_remote: pl.when(away)(lambda: copy().wait_send()))

    W = [s[f"W{f}"] for f in range(NF)]
    w_gather = []
    for f in range(NF):
        for k, at in tiles_of(f):
            n = tile_width(k) // 2
            W[f][0, at:at + n] = gw[128 * k:128 * k + n]
            W[f][0, at + n:at + 2 * n] = uw[128 * k:128 * k + n]
        w_gather.append(gather_start(W[f], "x", WIDTH[f] // 2))
    cot = s["cot"]
    cot[...] = cot_t[...].T

    def rows(f):
        return jnp.concatenate([W[f][j] for j in range(4)], axis=1)

    column = (z // 2 - a + 4) % 4
    z_sem = take(4 * NT)
    z_send = take(7 * NT)

    def z_dst(h, j):
        return X.at[h, :, :, pl.ds(pl.multiple_of((2 * j + c) * 128, 128), 128)]

    def z_copy(h, k):
        return pltpu.make_async_remote_copy(
            src_ref=held.at[:, pl.ds(h * TB, TB)], dst_ref=z_dst(h, column),
            send_sem=send.at[z_send + h * 7 + k - 1], recv_sem=recv.at[z_sem + 4 * h + column],
            device_id=dev(zz=(z + k) % 8), device_id_type=MESH,
        )

    @pl.when(is_sink)
    def _():
        for r in range(4):
            pltpu.make_async_copy(tok, held.at[r], recv.at[held_sem + r]).wait()
        for h in range(NT):
            pltpu.make_async_copy(
                held.at[:, pl.ds(h * TB, TB)], z_dst(h, column), recv.at[z_sem + 4 * h + column]
            ).start()
            for k in (1, 7, 2, 6, 3, 5, 4):
                z_copy(h, k).start()

    @functools.partial(leaving.append)
    def _():
        @pl.when(is_sink)
        def _():
            for h in range(NT):
                for k in range(1, 8):
                    z_copy(h, k).wait_send()

    def x_relay(h):
        copies = []
        for j in range(4):
            pltpu.make_async_copy(
                held.at[:, pl.ds(h * TB, TB)], z_dst(h, j), recv.at[z_sem + 4 * h + j]
            ).wait()
            copies.append(put(z_dst(h, j), z_dst(h, j), partner))
        return copies

    units = [(h, f) for h in range(NT) for f in range(NF)]
    pre_reduce, g_gather, w_reduce = {}, {}, {}

    def project(h, f):
        x = X[h].reshape(4 * TB, 1024)
        out = lax.dot_general(x, rows(f), (((1,), (1,)), ((), ())), preferred_element_type=f32)
        out = out.reshape(4, TB, WIDTH[f])
        s[f"own{f}"][h] = out[0]
        part, keep = s[f"part{f}"].at[h], s[f"keep{f}"].at[h]
        part[1] = out[2].astype(bf16)
        part[0, H:] = out[1, H:].astype(bf16)
        part[2, :H] = out[3, :H].astype(bf16)
        keep[0] = out[1, :H]
        keep[1] = out[3, H:]
        pre_reduce[h, f] = reduce_start(
            part, keep, s[f"midl{f}"].at[h], s[f"midr{f}"].at[h],
            s[f"finl{f}"].at[h], s[f"finr{f}"].at[h], "y", H,
        )

    def pointwise(gp, up, ct):
        sg = jax.nn.sigmoid(gp)
        cs = ct * sg
        return cs * up * (1.0 + gp * (1.0 - sg)), cs * gp

    def gate(h, f):
        reduce_finish(pre_reduce[h, f])
        pre = s[f"own{f}"][h] + s[f"finl{f}"][h].astype(f32) + s[f"finr{f}"][h].astype(f32)
        mine = slice(h * TB, h * TB + TB)
        G = s[f"G{f}"]
        for k, at in tiles_of(f):
            if k < 3:
                ct = cot[mine, 128 * k:128 * k + 128].astype(f32)
                gg, ug = pointwise(pre[:, at:at + 128], pre[:, at + 128:at + 256], ct)
                G[h, 0, :, at:at + 128] = gg.astype(bf16)
                G[h, 0, :, at + 128:at + 256] = ug.astype(bf16)
            else:
                ct = cot[mine, 384:448].astype(f32)
                ct = jnp.concatenate([ct, ct], axis=1)
                both = pre[:, at:at + 128]
                gg, ug = pointwise(both, pltpu.roll(both, 64, 1), ct)
                lane = lax.broadcasted_iota(jnp.int32, gg.shape, 1)
                G[h, 0, :, at:at + 128] = jnp.where(lane < 64, gg, pltpu.roll(ug, 64, 1)).astype(bf16)
        g_gather[h, f] = gather_start(G.at[h], "y", H)

    acc = s["acc"]

    def input_grad(h, f):
        gather_finish(g_gather[h, f])
        g = s[f"G{f}"][h].reshape(4 * TB, WIDTH[f])
        out = jnp.dot(g, rows(f), preferred_element_type=f32)
        for k in range(8):
            if f == 0:
                acc[h, k] = out[:, 128 * k:128 * k + 128]
            else:
                acc[h, k] += out[:, 128 * k:128 * k + 128]
        s[f"GT{f}"][:, 4 * TB * h:4 * TB * h + 4 * TB] = g.T

    core_recv, sink_send, sink_recv = (s[n] for n in ("cr", "zs", "zr"))
    core_copies = {}

    def dx_core(h):
        core_copies[h] = []
        for j in range(4):
            core_copies[h].append(put(acc.at[h, 2 * j + 1 - c], core_recv.at[h, j], partner))

    dx_sem = take(8 * NT)
    dx_send = take(4 * NT)

    def sink_copy(h, j):
        zj = 2 * ((a + j) % 4) + b // 2
        k = (z - zj + 8) % 8
        remote = pltpu.make_async_remote_copy(
            src_ref=sink_send.at[h, j], dst_ref=sink_recv.at[h, k],
            send_sem=send.at[dx_send + 4 * h + j], recv_sem=recv.at[dx_sem + 8 * h + k],
            device_id=dev(zz=zj), device_id_type=MESH,
        )
        return zj, remote

    def dx_sinks(h):
        for j in range(4):
            core_copies[h][j].wait_recv()
            sink_send[h, j] = (acc[h, 2 * j + c] + core_recv[h, j]).astype(bf16)
            zj, remote = sink_copy(h, j)

            @pl.when(zj == z)
            def _():
                pltpu.make_async_copy(
                    sink_send.at[h, j], sink_recv.at[h, 0], recv.at[dx_sem + 8 * h]
                ).start()

            @pl.when(zj != z)
            def _():
                remote.start()

            leaving.append(lambda zj=zj, copy=remote: pl.when(zj != z)(lambda: copy.wait_send()))

    last_send, last_recv = s["ls"], s["lr"]
    out_sem = take(2 * NT)
    out_send = take(4 * NT)

    def out_copy(h, r):
        return pltpu.make_async_remote_copy(
            src_ref=last_send.at[h, pl.ds(r * TB, TB)], dst_ref=last_recv.at[h, w],
            send_sem=send.at[out_send + 4 * h + r], recv_sem=recv.at[out_sem + 2 * h + w],
            device_id=dev(y=(b + r) % 4, ww=b % 2), device_id_type=MESH,
        )

    def dx_spread(h):
        @pl.when(is_sink)
        def _():
            total = None
            for k in range(8):
                pltpu.make_async_copy(
                    sink_send.at[h, 0], sink_recv.at[h, k], recv.at[dx_sem + 8 * h + k]
                ).wait()
                term = sink_recv[h, k].astype(f32)
                total = term if total is None else total + term
            last_send[h] = total
            for r in range(4):
                if r:
                    out_copy(h, r).start()
                else:
                    @pl.when(w == b % 2)
                    def _():
                        pltpu.make_async_copy(
                            last_send.at[h, pl.ds(0, TB)], last_recv.at[h, w],
                            recv.at[out_sem + 2 * h + w],
                        ).start()

                    @pl.when(w != b % 2)
                    def _():
                        out_copy(h, 0).start()

        @functools.partial(leaving.append)
        def _():
            @pl.when(is_sink)
            def _():
                for r in range(1, 4):
                    out_copy(h, r).wait_send()

                @pl.when(w != b % 2)
                def _():
                    out_copy(h, 0).wait_send()

    def dx_finish(h):
        for ww in range(2):
            pltpu.make_async_copy(
                last_send.at[h, pl.ds(0, TB)], last_recv.at[h, ww], recv.at[out_sem + 2 * h + ww]
            ).wait()
        dx_out[h * TB:h * TB + TB] = (last_recv[h, 0] + last_recv[h, 1]).astype(bf16)

    def weight_grad(f):
        g, n = s[f"GT{f}"][...], WIDTH[f] // 2
        part, keep = s[f"wp{f}"], s[f"wk{f}"]
        for j in (2, 1, 3, 0):
            x = X[:, :, :, 256 * j:256 * j + 256].reshape(512, 256)
            out = jnp.dot(g, x, preferred_element_type=f32)
            if j == 2:
                part[1] = out.astype(bf16)
            elif j == 1:
                part[0, n:] = out[n:].astype(bf16)
                keep[0] = out[:n]
            elif j == 3:
                part[2, :n] = out[:n].astype(bf16)
                keep[1] = out[n:]
                w_reduce[f] = reduce_start(
                    part, keep, s[f"wml{f}"], s[f"wmr{f}"], s[f"wfl{f}"], s[f"wfr{f}"], "x", n
                )
            else:
                s[f"wo{f}"][...] = out

    def weight_finish(f):
        reduce_finish(w_reduce[f])
        total = s[f"wo{f}"][...] + s[f"wfl{f}"][...].astype(f32) + s[f"wfr{f}"][...].astype(f32)
        for k, at in tiles_of(f):
            n = tile_width(k) // 2
            gg_out[128 * k:128 * k + n] = total[at:at + n]
            ug_out[128 * k:128 * k + n] = total[at + n:at + 2 * n]

    def ready(copies):
        for copy in copies:
            copy.wait_recv()

    gather_relay(w_gather[0])
    x0 = x_relay(0)
    gather_relay(w_gather[1])
    gather_finish(w_gather[0])
    ready(x0)
    project(0, 0)
    gather_finish(w_gather[1])
    project(0, 1)
    reduce_relay(pre_reduce[0, 0])
    reduce_relay(pre_reduce[0, 1])
    x1 = x_relay(1)
    ready(x1)
    project(1, 0)
    project(1, 1)
    gate(0, 0)
    gate(0, 1)
    gather_relay(g_gather[0, 0])
    gather_relay(g_gather[0, 1])
    reduce_relay(pre_reduce[1, 0])
    reduce_relay(pre_reduce[1, 1])
    input_grad(0, 0)
    input_grad(0, 1)
    dx_core(0)
    gate(1, 0)
    dx_sinks(0)
    gate(1, 1)
    gather_relay(g_gather[1, 0])
    gather_relay(g_gather[1, 1])
    dx_spread(0)
    input_grad(1, 0)
    weight_grad(0)
    input_grad(1, 1)
    dx_core(1)
    weight_grad(1)
    dx_sinks(1)
    reduce_relay(w_reduce[0])
    dx_finish(0)
    reduce_relay(w_reduce[1])
    dx_spread(1)
    weight_finish(0)
    dx_finish(1)
    weight_finish(1)

    for wait in leaving:
        wait()


def scratch_shapes():
    V = pltpu.VMEM
    shapes = {
        "cot": V((128, 448), bf16),
        "held": V((4, 128, 128), bf16),
        "X": V((NT, 4, TB, 1024), bf16),
        "acc": V((NT, 8, 4 * TB, 128), f32),
        "cr": V((NT, 4, 4 * TB, 128), f32),
        "zs": V((NT, 4, 4 * TB, 128), bf16),
        "zr": V((NT, 8, 4 * TB, 128), bf16),
        "ls": V((NT, 4 * TB, 128), f32),
        "lr": V((NT, 2, TB, 128), f32),
    }
    for f in range(NF):
        n = WIDTH[f]
        shapes[f"W{f}"] = V((4, n, 256), bf16)
        shapes[f"G{f}"] = V((NT, 4, TB, n), bf16)
        shapes[f"GT{f}"] = V((n, 512), bf16)
        shapes[f"own{f}"] = V((NT, TB, n), f32)
        shapes[f"part{f}"] = V((NT, 3, TB, n), bf16)
        shapes[f"keep{f}"] = V((NT, 2, H, n), f32)
        shapes[f"midl{f}"] = V((NT, H, n), bf16)
        shapes[f"midr{f}"] = V((NT, H, n), bf16)
        shapes[f"finl{f}"] = V((NT, TB, n), bf16)
        shapes[f"finr{f}"] = V((NT, TB, n), bf16)
        shapes[f"wo{f}"] = V((n, 256), f32)
        shapes[f"wp{f}"] = V((3, n, 256), bf16)
        shapes[f"wk{f}"] = V((2, n // 2, 256), f32)
        shapes[f"wml{f}"] = V((n // 2, 256), bf16)
        shapes[f"wmr{f}"] = V((n // 2, 256), bf16)
        shapes[f"wfl{f}"] = V((n, 256), bf16)
        shapes[f"wfr{f}"] = V((n, 256), bf16)
    shapes["send"] = pltpu.SemaphoreType.DMA((SEMS,))
    shapes["recv"] = pltpu.SemaphoreType.DMA((SEMS,))
    return shapes


SCRATCH = scratch_shapes()


def gradients(tokens, cotangent, gate_weight, up_weight):
    vmem = pl.BlockSpec(memory_space=pltpu.VMEM)
    return pl.pallas_call(
        kernel,
        out_shape=(
            jax.ShapeDtypeStruct((128, 128), bf16),
            jax.ShapeDtypeStruct((448, 256), f32),
            jax.ShapeDtypeStruct((448, 256), f32),
        ),
        in_specs=[vmem] * 4,
        out_specs=(vmem,) * 3,
        scratch_shapes=list(SCRATCH.values()),
        compiler_params=pltpu.CompilerParams(
            collective_id=0, has_side_effects=True, vmem_limit_bytes=62 << 20
        ),
        cost_estimate=pl.CostEstimate(
            flops=2_818_572_288, bytes_accessed=2_000_000, transcendentals=57344
        ),
    )(tokens, cotangent, gate_weight, up_weight)


def shards(tokens, cotangent, gate_weight, up_weight, gate_first, up_first, gate_second, up_second):
    gate_weight, up_weight = gate_weight.T, up_weight.T
    input_grad, gate_wgrad, up_wgrad = gradients(tokens, cotangent.T, gate_weight, up_weight)
    gate = adam_update(gate_weight, gate_first.T, gate_second.T, gate_wgrad)
    up = adam_update(up_weight, up_first.T, up_second.T, up_wgrad)
    return input_grad, *(new.T for pair in zip(gate, up) for new in pair)


def solution(mesh):
    spec = P("local", "node")
    return jax.shard_map(
        shards, mesh=mesh, in_specs=(spec,) * 8, out_specs=(spec,) * 7, check_vma=False
    )
```

```python
import functools

import jax
import jax.numpy as jnp
from jax import lax
from jax.experimental import pallas as pl
from jax.experimental.pallas import tpu as pltpu
from jax.sharding import PartitionSpec as P

first_decay = 0.9
second_decay = 0.999
learn_rate = 0.001
adam_eps = 1e-08
step_count = 10

MESH = pl.DeviceIdType.MESH
bf16, f32 = jnp.bfloat16, jnp.float32

NT = 2
TB = 128 // NT
H = TB // 2
CHUNKS = ((0, 1), (2, 3))
NF = len(CHUNKS)
SEMS = 256


def tile_width(k):
    return 256 if k < 3 else 128


WIDTH = tuple(sum(tile_width(k) for k in tiles) for tiles in CHUNKS)


def adam_update(weight, first, second, grad):
    first_new = first_decay * first.astype(jnp.float32) + (1.0 - first_decay) * grad
    second_new = second_decay * second.astype(jnp.float32) + (1.0 - second_decay) * grad * grad
    first_hat = first_new / (1.0 - first_decay**step_count)
    second_hat = second_new / (1.0 - second_decay**step_count)
    weight_new = weight.astype(jnp.float32) - learn_rate * first_hat / (
        jnp.sqrt(second_hat) + adam_eps
    )
    return (
        weight_new.astype(jnp.bfloat16),
        first_new.astype(jnp.bfloat16),
        second_new.astype(jnp.bfloat16),
    )


def tiles_of(f):
    at = 0
    for k in CHUNKS[f]:
        yield k, at
        at += tile_width(k)


def kernel(tok, cot_t, gw, uw, dx_out, gg_out, ug_out, *scratch):
    names = list(SCRATCH)
    s = dict(zip(names, scratch))
    send, recv = s["send"], s["recv"]
    node, local = lax.axis_index("node"), lax.axis_index("local")
    z, w, c = node // 4, (node // 2) % 2, node % 2
    a, b = local // 4, local % 4

    def dev(x=a, y=b, zz=z, ww=w, cc=c):
        return (zz * 4 + ww * 2 + cc, x * 4 + y)

    right = {"x": dev(x=(a + 1) % 4), "y": dev(y=(b + 1) % 4)}
    left = {"x": dev(x=(a + 3) % 4), "y": dev(y=(b + 3) % 4)}
    partner = dev(cc=1 - c)
    is_sink = (z % 2) == (b // 2)

    count = [0]
    leaving = []

    def take(n=1):
        at = count[0]
        count[0] += n
        assert count[0] <= SEMS
        return at

    def put(src, dst, to, sem=None, sem_at=None):
        i = take() if sem is None else sem
        j = i if sem_at is None else sem_at
        copy = pltpu.make_async_remote_copy(
            src_ref=src, dst_ref=dst, send_sem=send.at[i], recv_sem=recv.at[j],
            device_id=to, device_id_type=MESH,
        )
        copy.start()
        leaving.append(copy.wait_send)
        return copy

    def gather_start(buf, axis, half):
        lo, hi = pl.ds(0, half), pl.ds(half, half)
        r1 = put(buf.at[0, lo], buf.at[3, lo], right[axis])
        l1 = put(buf.at[0, hi], buf.at[1, hi], left[axis])
        r2 = put(buf.at[0, hi], buf.at[3, hi], right[axis])
        l2 = put(buf.at[0, lo], buf.at[1, lo], left[axis])
        return [buf, axis, half, r1, l1, r2, l2]

    def gather_relay(g):
        buf, axis, half, r1, l1, r2, l2 = g
        lo, hi = pl.ds(0, half), pl.ds(half, half)
        r1.wait_recv()
        r3 = put(buf.at[3, lo], buf.at[2, lo], right[axis])
        l1.wait_recv()
        l3 = put(buf.at[1, hi], buf.at[2, hi], left[axis])
        g += [r3, l3]

    def gather_finish(g):
        for copy in g[5:]:
            copy.wait_recv()

    def reduce_start(part, keep, mid_left, mid_right, from_left, from_right, axis, half):
        lo, hi = pl.ds(0, half), pl.ds(half, half)
        r1 = put(part.at[1, lo], mid_left, right[axis])
        l1 = put(part.at[1, hi], mid_right, left[axis])
        r2 = put(part.at[0, hi], from_left.at[hi], right[axis])
        l2 = put(part.at[2, lo], from_right.at[lo], left[axis])
        return [part, keep, mid_left, mid_right, from_left, from_right, axis, half, r1, l1, r2, l2]

    def reduce_relay(g):
        part, keep, mid_left, mid_right, from_left, from_right, axis, half, r1, l1, r2, l2 = g
        lo, hi = pl.ds(0, half), pl.ds(half, half)
        r1.wait_recv()
        part[0, :half] = (keep[0] + mid_left[...].astype(f32)).astype(bf16)
        r3 = put(part.at[0, lo], from_left.at[lo], right[axis])
        l1.wait_recv()
        part[2, half:] = (keep[1] + mid_right[...].astype(f32)).astype(bf16)
        l3 = put(part.at[2, hi], from_right.at[hi], left[axis])
        g += [r3, l3]

    def reduce_finish(g):
        for copy in g[10:]:
            copy.wait_recv()

    W = [s[f"W{f}"] for f in range(NF)]
    loads = []
    for f in range(NF):
        copies = []
        for k, at in tiles_of(f):
            n = tile_width(k) // 2
            for ref, to in ((gw, at), (uw, at + n)):
                copy = pltpu.make_async_copy(
                    ref.at[pl.ds(128 * k, n)], W[f].at[0, pl.ds(to, n)], recv.at[take()]
                )
                copy.start()
                copies.append(copy)
        loads.append(copies)
    loads.append(pltpu.make_async_copy(cot_t, s["cot_t"], recv.at[take()]))
    loads[NF].start()

    peers = [right["x"], left["x"], partner]
    peers += [dev(zz=(z + k) % 8) for k in range(1, 8)]
    peers += [dev(y=(b + k) % 4, ww=w) for k in range(1, 4)]
    peers += [dev(y=(b + k) % 4, ww=1 - w) for k in range(4)]
    barrier = pltpu.get_barrier_semaphore()
    for peer in peers:
        pl.semaphore_signal(barrier, inc=1, device_id=peer, device_id_type=MESH)
    pl.semaphore_wait(barrier, len(peers))

    held, X = s["held"], s["X"]
    home = 2 * (z % 2) + w
    slot = (b - home + 4) % 4
    held_sem = take(4)
    tok_sem = take(2)
    for wd in range(2):
        own = (home == b) & (w == wd)
        away = jnp.logical_not(own)

        def tok_remote(to=dev(y=home, ww=wd), i=tok_sem + wd):
            return pltpu.make_async_remote_copy(
                src_ref=tok, dst_ref=held.at[slot], send_sem=send.at[i],
                recv_sem=recv.at[held_sem + slot], device_id=to, device_id_type=MESH,
            )

        @pl.when(own)
        def _():
            pltpu.make_async_copy(tok, held.at[0], recv.at[held_sem]).start()

        @pl.when(away)
        def _():
            tok_remote().start()

        leaving.append(lambda away=away, copy=tok_remote: pl.when(away)(lambda: copy().wait_send()))

    w_gather = []
    for f in range(NF):
        for copy in loads[f]:
            copy.wait()
        w_gather.append(gather_start(W[f], "x", WIDTH[f] // 2))
    cot = s["cot"]
    loads[NF].wait()
    cot[...] = s["cot_t"][...].T

    def rows(f):
        return jnp.concatenate([W[f][j] for j in range(4)], axis=1)

    def column_of(dz):
        return ((z + dz + 8) % 8 // 2 - a + 4) % 4

    column = column_of(0)
    z_sem, far_sem, core_sem = take(4 * NT), take(2 * NT), take(4 * NT)
    z_send, pass_send, core_send = take(4 * NT), take(4 * NT), take(4 * NT)
    STEPS = (2, -2, 1, -1)

    def z_dst(h, j):
        return X.at[h, :, :, pl.ds(pl.multiple_of((2 * j + c) * 128, 128), 128)]

    def z_half(h, j, half):
        return X.at[h, pl.ds(2 * half, 2), :, pl.ds(pl.multiple_of((2 * j + c) * 128, 128), 128)]

    def z_copy(h, q):
        return pltpu.make_async_remote_copy(
            src_ref=held.at[:, pl.ds(h * TB, TB)], dst_ref=z_dst(h, column),
            send_sem=send.at[z_send + 4 * h + q], recv_sem=recv.at[z_sem + 4 * h + column],
            device_id=dev(zz=(z + STEPS[q] + 8) % 8), device_id_type=MESH,
        )

    def pass_copies(h, side):
        j = column_of(2 * side)
        q = pass_send + 4 * h + side + 1
        half = (side + 1) // 2
        return [
            pltpu.make_async_remote_copy(
                src_ref=z_dst(h, j), dst_ref=z_dst(h, j),
                send_sem=send.at[q], recv_sem=recv.at[z_sem + 4 * h + j],
                device_id=dev(zz=(z - side + 8) % 8), device_id_type=MESH,
            ),
            pltpu.make_async_remote_copy(
                src_ref=z_half(h, j, half), dst_ref=z_half(h, j, half),
                send_sem=send.at[q + 1], recv_sem=recv.at[far_sem + 2 * h + half],
                device_id=dev(zz=(z - 2 * side + 8) % 8), device_id_type=MESH,
            ),
        ]

    def z_wait(h, j):
        pltpu.make_async_copy(
            held.at[:, pl.ds(h * TB, TB)], z_dst(h, j), recv.at[z_sem + 4 * h + j]
        ).wait()

    def core_copy(h, q, j):
        return pltpu.make_async_remote_copy(
            src_ref=z_dst(h, j), dst_ref=z_dst(h, j), send_sem=send.at[core_send + 4 * h + q],
            recv_sem=recv.at[core_sem + 4 * h + j], device_id=partner, device_id_type=MESH,
        )

    @pl.when(is_sink)
    def _():
        for r in range(4):
            pltpu.make_async_copy(tok, held.at[r], recv.at[held_sem + r]).wait()
        for h in range(NT):
            for q in range(4):
                z_copy(h, q).start()
            pltpu.make_async_copy(
                held.at[:, pl.ds(h * TB, TB)], z_dst(h, column), recv.at[z_sem + 4 * h + column]
            ).start()

    def x_near(h):
        @pl.when(is_sink)
        def _():
            for q, side in enumerate((-1, 1)):
                z_wait(h, column_of(2 * side))
                for copy in pass_copies(h, side):
                    copy.start()
                core_copy(h, q, column_of(2 * side)).start()
            z_wait(h, column)
            core_copy(h, 2, column).start()

        @pl.when(jnp.logical_not(is_sink))
        def _():
            for q, side in enumerate((-1, 1)):
                z_wait(h, column_of(side))
                core_copy(h, q, column_of(side)).start()

    def x_far(h):
        @pl.when(is_sink)
        def _():
            j = column_of(4)
            for half in range(2):
                pltpu.make_async_copy(
                    held.at[pl.ds(0, 2), pl.ds(h * TB, TB)], z_half(h, j, half),
                    recv.at[far_sem + 2 * h + half],
                ).wait()
            core_copy(h, 3, j).start()

        @pl.when(jnp.logical_not(is_sink))
        def _():
            for q, side in enumerate((-3, 3)):
                z_wait(h, column_of(side))
                core_copy(h, 2 + q, column_of(side)).start()

    def x_ready(h):
        for j in range(4):
            core_copy(h, j, j).wait_recv()

    @functools.partial(leaving.append)
    def _():
        for h in range(NT):
            for q in range(4):
                core_copy(h, q, 0).wait_send()

        @pl.when(is_sink)
        def _():
            for h in range(NT):
                for q in range(4):
                    z_copy(h, q).wait_send()
                for side in (-1, 1):
                    for copy in pass_copies(h, side):
                        copy.wait_send()

    units = [(h, f) for h in range(NT) for f in range(NF)]
    pre_reduce, g_gather, w_reduce = {}, {}, {}

    def project(h, f):
        x = X[h].reshape(4 * TB, 1024)
        out = lax.dot_general(x, rows(f), (((1,), (1,)), ((), ())), preferred_element_type=f32)
        out = out.reshape(4, TB, WIDTH[f])
        s[f"own{f}"][h] = out[0]
        part, keep = s[f"part{f}"].at[h], s[f"keep{f}"].at[h]
        part[1] = out[2].astype(bf16)
        part[0, H:] = out[1, H:].astype(bf16)
        part[2, :H] = out[3, :H].astype(bf16)
        keep[0] = out[1, :H]
        keep[1] = out[3, H:]
        pre_reduce[h, f] = reduce_start(
            part, keep, s[f"midl{f}"].at[h], s[f"midr{f}"].at[h],
            s[f"finl{f}"].at[h], s[f"finr{f}"].at[h], "y", H,
        )

    def pointwise(gp, up, ct):
        sg = jax.nn.sigmoid(gp)
        cs = ct * sg
        return cs * up * (1.0 + gp * (1.0 - sg)), cs * gp

    def gate(h, f):
        reduce_finish(pre_reduce[h, f])
        pre = s[f"own{f}"][h] + s[f"finl{f}"][h].astype(f32) + s[f"finr{f}"][h].astype(f32)
        mine = slice(h * TB, h * TB + TB)
        G = s[f"G{f}"]
        for k, at in tiles_of(f):
            if k < 3:
                ct = cot[mine, 128 * k:128 * k + 128].astype(f32)
                gg, ug = pointwise(pre[:, at:at + 128], pre[:, at + 128:at + 256], ct)
                G[h, 0, :, at:at + 128] = gg.astype(bf16)
                G[h, 0, :, at + 128:at + 256] = ug.astype(bf16)
            else:
                ct = cot[mine, 384:448].astype(f32)
                ct = jnp.concatenate([ct, ct], axis=1)
                both = pre[:, at:at + 128]
                gg, ug = pointwise(both, pltpu.roll(both, 64, 1), ct)
                lane = lax.broadcasted_iota(jnp.int32, gg.shape, 1)
                G[h, 0, :, at:at + 128] = jnp.where(lane < 64, gg, pltpu.roll(ug, 64, 1)).astype(bf16)
        g_gather[h, f] = gather_start(G.at[h], "y", H)

    acc = s["acc"]

    def input_grad(h, f):
        gather_finish(g_gather[h, f])
        g = s[f"G{f}"][h].reshape(4 * TB, WIDTH[f])
        out = jnp.dot(g, rows(f), preferred_element_type=f32)
        for k in range(8):
            if f == 0:
                acc[h, k] = out[:, 128 * k:128 * k + 128]
            else:
                acc[h, k] += out[:, 128 * k:128 * k + 128]
        s[f"GT{f}"][:, 4 * TB * h:4 * TB * h + 4 * TB] = g.T

    core_recv, sink_send, sink_recv = (s[n] for n in ("cr", "zs", "zr"))
    core_copies = {}

    def dx_core(h):
        core_copies[h] = []
        for j in range(4):
            core_copies[h].append(put(acc.at[h, 2 * j + 1 - c], core_recv.at[h, j], partner))

    dx_sem = take(8 * NT)
    dx_send = take(4 * NT)

    def sink_copy(h, j):
        zj = 2 * ((a + j) % 4) + b // 2
        k = (z - zj + 8) % 8
        remote = pltpu.make_async_remote_copy(
            src_ref=sink_send.at[h, j], dst_ref=sink_recv.at[h, k],
            send_sem=send.at[dx_send + 4 * h + j], recv_sem=recv.at[dx_sem + 8 * h + k],
            device_id=dev(zz=zj), device_id_type=MESH,
        )
        return zj, remote

    def dx_sinks(h):
        for j in range(4):
            core_copies[h][j].wait_recv()
            sink_send[h, j] = (acc[h, 2 * j + c] + core_recv[h, j]).astype(bf16)
            zj, remote = sink_copy(h, j)

            @pl.when(zj == z)
            def _():
                pltpu.make_async_copy(
                    sink_send.at[h, j], sink_recv.at[h, 0], recv.at[dx_sem + 8 * h]
                ).start()

            @pl.when(zj != z)
            def _():
                remote.start()

            leaving.append(lambda zj=zj, copy=remote: pl.when(zj != z)(lambda: copy.wait_send()))

    last_send, last_recv = s["ls"], s["lr"]
    out_sem = take(2 * NT)
    out_send = take(4 * NT)

    def out_copy(h, r):
        return pltpu.make_async_remote_copy(
            src_ref=last_send.at[h, pl.ds(r * TB, TB)], dst_ref=last_recv.at[h, w],
            send_sem=send.at[out_send + 4 * h + r], recv_sem=recv.at[out_sem + 2 * h + w],
            device_id=dev(y=(b + r) % 4, ww=b % 2), device_id_type=MESH,
        )

    def dx_spread(h):
        @pl.when(is_sink)
        def _():
            total = None
            for k in range(8):
                pltpu.make_async_copy(
                    sink_send.at[h, 0], sink_recv.at[h, k], recv.at[dx_sem + 8 * h + k]
                ).wait()
                term = sink_recv[h, k].astype(f32)
                total = term if total is None else total + term
            last_send[h] = total
            for r in range(4):
                if r:
                    out_copy(h, r).start()
                else:
                    @pl.when(w == b % 2)
                    def _():
                        pltpu.make_async_copy(
                            last_send.at[h, pl.ds(0, TB)], last_recv.at[h, w],
                            recv.at[out_sem + 2 * h + w],
                        ).start()

                    @pl.when(w != b % 2)
                    def _():
                        out_copy(h, 0).start()

        @functools.partial(leaving.append)
        def _():
            @pl.when(is_sink)
            def _():
                for r in range(1, 4):
                    out_copy(h, r).wait_send()

                @pl.when(w != b % 2)
                def _():
                    out_copy(h, 0).wait_send()

    def dx_finish(h):
        for ww in range(2):
            pltpu.make_async_copy(
                last_send.at[h, pl.ds(0, TB)], last_recv.at[h, ww], recv.at[out_sem + 2 * h + ww]
            ).wait()
        dx_out[h * TB:h * TB + TB] = (last_recv[h, 0] + last_recv[h, 1]).astype(bf16)

    def weight_grad(f):
        g, n = s[f"GT{f}"][...], WIDTH[f] // 2
        part, keep = s[f"wp{f}"], s[f"wk{f}"]
        for j in (2, 1, 3, 0):
            x = X[:, :, :, 256 * j:256 * j + 256].reshape(512, 256)
            out = jnp.dot(g, x, preferred_element_type=f32)
            if j == 2:
                part[1] = out.astype(bf16)
            elif j == 1:
                part[0, n:] = out[n:].astype(bf16)
                keep[0] = out[:n]
            elif j == 3:
                part[2, :n] = out[:n].astype(bf16)
                keep[1] = out[n:]
                w_reduce[f] = reduce_start(
                    part, keep, s[f"wml{f}"], s[f"wmr{f}"], s[f"wfl{f}"], s[f"wfr{f}"], "x", n
                )
            else:
                s[f"wo{f}"][...] = out

    def weight_finish(f):
        reduce_finish(w_reduce[f])
        total = s[f"wo{f}"][...] + s[f"wfl{f}"][...].astype(f32) + s[f"wfr{f}"][...].astype(f32)
        for k, at in tiles_of(f):
            n = tile_width(k) // 2
            gg_out[128 * k:128 * k + n] = total[at:at + n]
            ug_out[128 * k:128 * k + n] = total[at + n:at + 2 * n]

    gather_relay(w_gather[0])
    x_near(0)
    x_far(0)
    x_near(1)
    gather_relay(w_gather[1])
    gather_finish(w_gather[0])
    x_ready(0)
    project(0, 0)
    gather_finish(w_gather[1])
    project(0, 1)
    x_far(1)
    reduce_relay(pre_reduce[0, 0])
    reduce_relay(pre_reduce[0, 1])
    x_ready(1)
    project(1, 0)
    project(1, 1)
    gate(0, 0)
    gate(0, 1)
    gather_relay(g_gather[0, 0])
    gather_relay(g_gather[0, 1])
    reduce_relay(pre_reduce[1, 0])
    reduce_relay(pre_reduce[1, 1])
    input_grad(0, 0)
    input_grad(0, 1)
    dx_core(0)
    gate(1, 0)
    dx_sinks(0)
    gate(1, 1)
    gather_relay(g_gather[1, 0])
    gather_relay(g_gather[1, 1])
    dx_spread(0)
    input_grad(1, 0)
    weight_grad(0)
    input_grad(1, 1)
    dx_core(1)
    weight_grad(1)
    dx_sinks(1)
    reduce_relay(w_reduce[0])
    dx_finish(0)
    reduce_relay(w_reduce[1])
    dx_spread(1)
    weight_finish(0)
    dx_finish(1)
    weight_finish(1)

    for wait in leaving:
        wait()


def scratch_shapes():
    V = pltpu.VMEM
    shapes = {
        "cot": V((128, 448), bf16),
        "cot_t": V((448, 128), bf16),
        "held": V((4, 128, 128), bf16),
        "X": V((NT, 4, TB, 1024), bf16),
        "acc": V((NT, 8, 4 * TB, 128), f32),
        "cr": V((NT, 4, 4 * TB, 128), f32),
        "zs": V((NT, 4, 4 * TB, 128), bf16),
        "zr": V((NT, 8, 4 * TB, 128), bf16),
        "ls": V((NT, 4 * TB, 128), f32),
        "lr": V((NT, 2, TB, 128), f32),
    }
    for f in range(NF):
        n = WIDTH[f]
        shapes[f"W{f}"] = V((4, n, 256), bf16)
        shapes[f"G{f}"] = V((NT, 4, TB, n), bf16)
        shapes[f"GT{f}"] = V((n, 512), bf16)
        shapes[f"own{f}"] = V((NT, TB, n), f32)
        shapes[f"part{f}"] = V((NT, 3, TB, n), bf16)
        shapes[f"keep{f}"] = V((NT, 2, H, n), f32)
        shapes[f"midl{f}"] = V((NT, H, n), bf16)
        shapes[f"midr{f}"] = V((NT, H, n), bf16)
        shapes[f"finl{f}"] = V((NT, TB, n), bf16)
        shapes[f"finr{f}"] = V((NT, TB, n), bf16)
        shapes[f"wo{f}"] = V((n, 256), f32)
        shapes[f"wp{f}"] = V((3, n, 256), bf16)
        shapes[f"wk{f}"] = V((2, n // 2, 256), f32)
        shapes[f"wml{f}"] = V((n // 2, 256), bf16)
        shapes[f"wmr{f}"] = V((n // 2, 256), bf16)
        shapes[f"wfl{f}"] = V((n, 256), bf16)
        shapes[f"wfr{f}"] = V((n, 256), bf16)
    shapes["send"] = pltpu.SemaphoreType.DMA((SEMS,))
    shapes["recv"] = pltpu.SemaphoreType.DMA((SEMS,))
    return shapes


SCRATCH = scratch_shapes()


def gradients(tokens, cotangent, gate_weight, up_weight):
    vmem = pl.BlockSpec(memory_space=pltpu.VMEM)
    return pl.pallas_call(
        kernel,
        out_shape=(
            jax.ShapeDtypeStruct((128, 128), bf16),
            jax.ShapeDtypeStruct((448, 256), f32),
            jax.ShapeDtypeStruct((448, 256), f32),
        ),
        in_specs=[pl.BlockSpec(memory_space=pltpu.HBM)] * 4,
        out_specs=(vmem,) * 3,
        scratch_shapes=list(SCRATCH.values()),
        compiler_params=pltpu.CompilerParams(
            collective_id=0, has_side_effects=True, vmem_limit_bytes=62 << 20
        ),
        cost_estimate=pl.CostEstimate(
            flops=2_818_572_288, bytes_accessed=2_000_000, transcendentals=57344
        ),
    )(tokens, cotangent, gate_weight, up_weight)


def shards(tokens, cotangent, gate_weight, up_weight, gate_first, up_first, gate_second, up_second):
    gate_weight, up_weight = gate_weight.T, up_weight.T
    input_grad, gate_wgrad, up_wgrad = gradients(tokens, cotangent.T, gate_weight, up_weight)
    gate = adam_update(gate_weight, gate_first.T, gate_second.T, gate_wgrad)
    up = adam_update(up_weight, up_first.T, up_second.T, up_wgrad)
    return input_grad, *(new.T for pair in zip(gate, up) for new in pair)


def solution(mesh):
    spec = P("local", "node")
    return jax.shard_map(
        shards, mesh=mesh, in_specs=(spec,) * 8, out_specs=(spec,) * 7, check_vma=False
    )
```
